256 devices in a mesh: dp: 128 (over z, x, y_lo, core), mp: 2 (over y_hi).
Axes of the slice: x: 4, y: 4 (y_hi: 2, y_lo: 2; y = y_hi * 2 + y_lo), z: 8, core: 2. Of those that a mesh axis runs over, the one named last changes fastest.
Arguments:
- images: bfloat16 [16384, 1152], P('dp', 'mp'), may hold values from -0.1796875 to 0.1796875
- text_feats: bfloat16 [16384, 1152], P('dp', 'mp'), may hold values from -0.1796875 to 0.1796875
- projection: bfloat16 [1152, 1152], P('mp'), may hold values from -0.1875 to 0.1875
- ranks: int32 [16384], P('dp'), may hold values from 0 to 16383, each once
Outputs:
- grad_image: float32 [16384, 1152], P('dp', 'mp')
- grad_text: float32 [16384, 1152], P('dp', 'mp')
- grad_weight: float32 [1152, 1152], P('mp')
The draws below stay inside these ranges and needn't reach their ends.
Inputs may be any that keep to these rules, and one draw needn't show every extreme that they name: `ranks`: each of 0 to 16383 appears once.
All inputs are finite; a program needn't handle non-finite values.
Results may differ from the reference program's by a relative error of at most 0.015.
Values may be sent and summed in bfloat16 or wider, within the bound.
No kernel may reach another device: no remote copies, remote signals or barrier semaphores. Data moves between devices by JAX's collectives and lax.ppermute only.
A program may use at most 192 MiB of HBM per device.

```python
import jax
import jax.numpy as jnp
from jax import lax

E = 1152
ROWS = 128
BATCH = 16384


def steps_of(stream_key, extent, cuts, low, high):
    level = 1.0
    for dim, shards_of in cuts:
        heights = jax.random.uniform(jax.random.fold_in(jax.random.fold_in(stream_key, 6), dim), (shards_of,), jnp.float32, low / len(cuts), high / len(cuts))
        level = level * jnp.repeat(jnp.exp(heights), extent[dim] // shards_of).reshape((-1,) + (1,) * (len(extent) - 1 - dim))
    return level


def noise(own_key, extent, spread, most, cuts=(), held_as=jnp.bfloat16):
    result = spread * jax.random.normal(own_key, extent, jnp.float32)
    if cuts:
        result = result * steps_of(own_key, extent, cuts, -0.22, 0.18)
    return jnp.clip(result, -most, most).astype(held_as)


def setup_inputs(seed: int = 0) -> dict:
    keys = jax.random.split(jax.random.key(seed), 5)
    return {
        "images": noise(keys[0], (BATCH, E), 0.03, 0.1796875, ((0, 128), (1, 2))),
        "text_feats": noise(keys[1], (BATCH, E), 0.03, 0.1796875, ((0, 128), (1, 2))),
        "projection": noise(keys[2], (E, E), E ** -0.5, 0.1875, ((0, 2),)),
        "ranks": jax.random.permutation(keys[3], BATCH).astype(jnp.int32),
    }


def reference(images, text_feats, projection, ranks):
    batch = images.shape[0]
    weight = (0.5 + 1.5 * ranks.astype(jnp.float32) / (batch - 1)).astype(jnp.bfloat16)
    weight32 = weight.astype(jnp.float32)
    text_out = jnp.dot(text_feats, projection, preferred_element_type=jnp.float32)
    img32 = images.astype(jnp.float32)
    inv_img = lax.rsqrt(lax.optimization_barrier(jnp.sum(img32 * img32, axis=1)) + 1e-06)
    inv_txt = lax.rsqrt(lax.optimization_barrier(jnp.sum(text_out * text_out, axis=1)) + 1e-06)
    unit_img = img32 * inv_img[:, None]
    unit_txt = text_out * inv_txt[:, None]
    img_b = unit_img.astype(jnp.bfloat16)
    txt_b = unit_txt.astype(jnp.bfloat16)
    blocks = batch // ROWS
    columns = jnp.arange(batch, dtype=jnp.int32)

    def step(carry, index):
        start = (index * ROWS).astype(jnp.int32)
        block_img = lax.dynamic_slice_in_dim(img_b, start, ROWS, 0)
        block_w = lax.dynamic_slice_in_dim(weight32, start, ROWS, 0)
        logits = 10.0 * jnp.dot(block_img, txt_b.T, preferred_element_type=jnp.float32) - 2.0
        rows_here = start + jnp.arange(ROWS, dtype=jnp.int32)
        diag = (rows_here[:, None] == columns[None, :]).astype(jnp.float32)
        coef = (block_w[:, None] * weight32[None, :] * 10.0 * (jax.nn.sigmoid(logits) - diag)).astype(jnp.bfloat16)
        grad_block = jnp.dot(coef, txt_b, preferred_element_type=jnp.float32)
        carry = carry + jnp.dot(coef.T, block_img, preferred_element_type=jnp.float32)
        return (carry, grad_block)
    init = jnp.zeros((batch, images.shape[1]), jnp.float32)
    grad_utxt, pieces = lax.scan(step, init, jnp.arange(blocks, dtype=jnp.int32))
    grad_uimg = pieces.reshape(batch, images.shape[1])
    img_dot = lax.optimization_barrier(jnp.sum(unit_img * grad_uimg, axis=1))
    txt_dot = lax.optimization_barrier(jnp.sum(unit_txt * grad_utxt, axis=1))
    grad_image = (grad_uimg - unit_img * img_dot[:, None]) * inv_img[:, None]
    grad_out = ((grad_utxt - unit_txt * txt_dot[:, None]) * inv_txt[:, None]).astype(jnp.bfloat16)
    grad_text = jnp.dot(grad_out, projection.T, preferred_element_type=jnp.float32)
    grad_weight = jnp.dot(text_feats.T, grad_out, preferred_element_type=jnp.float32)
    return (grad_image, grad_text, grad_weight)
```

```python
import jax
import jax.numpy as jnp
from jax import lax
from jax.sharding import Mesh
from jax.sharding import PartitionSpec as P

FINE = ("z", "x", "yl", "c", "yh")
SIZES = (8, 4, 2, 2, 2)
DP = ("z", "x", "yl", "c")
IMG = ("z", "c")
TXT = ("x", "yl", "yh")
SWAP = [(0, 1), (1, 0)]
BF = jnp.bfloat16
F32 = jnp.float32


def contract(left, right, dims):
    return lax.dot_general(left, right, ((dims[:1], dims[1:]), ((), ())), preferred_element_type=F32)


def spread(block, axes, count):
    copies = jnp.broadcast_to(block[None], (count,) + block.shape)
    return lax.all_to_all(copies, axes, 0, 0)


def gather_sum(parts, axes):
    got = lax.all_to_all(parts, axes, 0, 0)
    return jnp.sum(got.astype(F32), axis=0)


def on_device(images, text_feats, projection, ranks):
    rows, half = images.shape
    own = rows // 2
    width = 2 * half
    n_dp = 128
    batch = rows * n_dp
    low = lax.axis_index("yh") == 0

    weight = (0.5 + 1.5 * ranks.astype(F32) / (batch - 1)).astype(BF)
    weight = jnp.where(low, weight[:own], weight[own:])
    partial = jnp.dot(text_feats, projection, preferred_element_type=F32)
    send = jnp.concatenate(
        [
            jnp.where(low, images[own:], images[:own]),
            jnp.where(low, partial[own:], partial[:own]).astype(BF),
        ],
        axis=1,
    )
    got = lax.ppermute(send, "yh", SWAP)
    text_out = jnp.where(low, partial[:own], partial[own:]) + got[:, half:].astype(F32)
    img_own = jnp.where(low, images[:own], images[own:])
    img_got = got[:, :half]
    img32 = jnp.concatenate(
        [jnp.where(low, img_own, img_got), jnp.where(low, img_got, img_own)], axis=1
    ).astype(F32)
    inv_img = lax.rsqrt(jnp.sum(img32 * img32, axis=1, keepdims=True) + 1e-06)
    inv_txt = lax.rsqrt(jnp.sum(text_out * text_out, axis=1, keepdims=True) + 1e-06)
    unit_img = img32 * inv_img
    unit_txt = text_out * inv_txt
    img_b = unit_img.astype(BF)
    txt_b = unit_txt.astype(BF)

    column = jnp.pad(weight[:, None], ((0, 0), (0, 127)))
    all_img = lax.all_gather(jnp.concatenate([img_b, column], axis=1), IMG, axis=0, tiled=True)
    all_txt = spread(jnp.concatenate([txt_b, column], axis=1), TXT, 16).reshape(16 * own, width + 128)

    blk_img, w_img = all_img[:, :width], all_img[:, width:]
    blk_txt, w_txt = all_txt[:, :width], all_txt[:, width:]
    logits = 10.0 * contract(blk_img, blk_txt, (1, 1)) - 2.0
    pair = w_img[:, :1].astype(F32) * w_txt[:, 0].astype(F32)[None, :]
    coef = (pair * 10.0 * jax.nn.sigmoid(logits)).astype(BF)
    part_img = jnp.dot(coef, blk_txt, preferred_element_type=F32).astype(BF)
    part_txt = contract(coef, blk_img, (0, 0)).astype(BF)

    w32 = weight.astype(F32)[:, None]
    diag = 10.0 * w32 * w32
    grad_utxt = gather_sum(part_txt.reshape(16, own, width), TXT) - diag * img_b.astype(F32)
    txt_dot = jnp.sum(unit_txt * grad_utxt, axis=1, keepdims=True)
    grad_out = ((grad_utxt - unit_txt * txt_dot) * inv_txt).astype(BF)
    other = lax.ppermute(grad_out, "yh", SWAP)
    grad_full = jnp.concatenate(
        [jnp.where(low, grad_out, other), jnp.where(low, other, grad_out)], axis=0
    )
    weight_part = contract(text_feats, grad_full, (0, 0)).astype(BF)
    grad_text = contract(grad_full, projection, (1, 1))

    tiles = weight_part.reshape(half // 8, 8, width // 128, 128).transpose(0, 2, 1, 3)
    tiles = tiles.reshape(-1, 8, 128)
    n_tiles = tiles.shape[0]
    share = -(-n_tiles // n_dp)
    tiles = jnp.pad(tiles, ((0, share * n_dp - n_tiles), (0, 0), (0, 0)))
    mine = gather_sum(tiles.reshape(n_dp, share, 8, 128), DP).astype(BF)
    whole = spread(mine, DP, n_dp).reshape(-1, 8, 128)[:n_tiles]
    grad_weight = (
        whole.reshape(half // 8, width // 128, 8, 128).transpose(0, 2, 1, 3).reshape(half, width)
    ).astype(F32)

    grad_uimg = lax.psum_scatter(part_img, IMG, scatter_dimension=0, tiled=True).astype(F32)
    grad_uimg = grad_uimg - diag * txt_b.astype(F32)
    img_dot = jnp.sum(unit_img * grad_uimg, axis=1, keepdims=True)
    grad_img = (grad_uimg - unit_img * img_dot) * inv_img
    left, right = grad_img[:, :half], grad_img[:, half:]
    back = lax.ppermute(jnp.where(low, right, left).astype(BF), "yh", SWAP).astype(F32)
    keep = jnp.where(low, left, right)
    grad_image = jnp.concatenate(
        [jnp.where(low, keep, back), jnp.where(low, back, keep)], axis=0
    )
    return (grad_image, grad_text, grad_weight)


def solution(mesh):
    fine = Mesh(mesh.devices.reshape(SIZES), FINE)
    return jax.shard_map(
        on_device,
        mesh=fine,
        in_specs=(P(DP, "yh"), P(DP, "yh"), P("yh", None), P(DP)),
        out_specs=(P(DP, "yh"), P(DP, "yh"), P("yh", None)),
        check_vma=False,
    )
```

```python
import jax
import jax.numpy as jnp
from jax import lax
from jax.sharding import Mesh
from jax.sharding import PartitionSpec as P

FINE = ("z", "x", "yl", "c", "yh")
SIZES = (8, 4, 2, 2, 2)
DP = ("z", "x", "yl", "c")
NEAR = ("x", "yl")
SWAP = [(0, 1), (1, 0)]
BF = jnp.bfloat16
F32 = jnp.float32


def contract(left, right, dims):
    return lax.dot_general(left, right, ((dims[:1], dims[1:]), ((), ())), preferred_element_type=F32)


def spread(block, axes, count):
    copies = jnp.broadcast_to(block[None], (count,) + block.shape)
    return lax.all_to_all(copies, axes, 0, 0)


def summed(got):
    return jnp.sum(got.astype(F32), axis=0)


def z_ring(block):
    n = SIZES[0]
    up = [(i, (i + 1) % n) for i in range(n)]
    down = [(i, (i - 1) % n) for i in range(n)]
    held = [None] * n
    held[0] = fro = to = block
    for step in range(1, n // 2):
        fro = held[n - step] = lax.ppermute(fro, "z", up)
        to = held[step] = lax.ppermute(to, "z", down)
    cut = block.shape[0] // 16 * 8
    held[n // 2] = jnp.concatenate(
        [lax.ppermute(fro[:cut], "z", up), lax.ppermute(to[cut:], "z", down)], axis=0
    )
    return held


def weight_row(weight, width):
    return jnp.pad(weight[None], ((0, 7), (0, width - weight.shape[0])))


def on_device(images, text_feats, projection, ranks):
    rows, half = images.shape
    own = rows // 2
    width = 2 * half
    batch = rows * 128
    nz, near = 8, 8
    yh = lax.axis_index("yh")
    low = yh == 0
    first = lax.axis_index("c") == 0
    place = lax.axis_index("x") * 2 + lax.axis_index("yl")

    def side(array):
        return jnp.where(low, array[:own], array[own:])

    weight = (0.5 + 1.5 * ranks.astype(F32) / (batch - 1)).astype(BF)

    img_other = lax.ppermute(images, "yh", SWAP)
    partial = jnp.dot(text_feats, projection, preferred_element_type=F32)
    got = lax.ppermute(
        jnp.where(low, partial[own:], partial[:own]).astype(BF), "yh", SWAP
    )
    img32 = jnp.concatenate(
        [jnp.where(low, images, img_other), jnp.where(low, img_other, images)], axis=1
    ).astype(F32)
    inv_img = lax.rsqrt(jnp.sum(img32 * img32, axis=1, keepdims=True) + 1e-06)
    img_b = (img32 * inv_img).astype(BF)
    held = z_ring(jnp.concatenate([img_b, weight_row(weight, width)], axis=0))

    text_out = side(partial) + got.astype(F32)
    inv_txt = lax.rsqrt(jnp.sum(text_out * text_out, axis=1, keepdims=True) + 1e-06)
    unit_txt = text_out * inv_txt
    txt_block = jnp.concatenate([unit_txt.astype(BF), weight_row(side(weight), width)], axis=0)
    txt_mine = spread(txt_block, NEAR, near)
    txt_theirs = lax.ppermute(txt_mine, "c", SWAP)

    all_img = jnp.concatenate([h[:rows] for h in held], axis=0)
    w_img = jnp.concatenate([h[rows, :rows] for h in held], axis=0).astype(F32)

    def pairs(txt, diagonal):
        blk = txt[:, :own].reshape(near * own, width)
        w_txt = txt[:, own, :own].reshape(near * own).astype(F32)
        logits = 10.0 * contract(all_img, blk, (1, 1)) - 2.0
        sig = jax.nn.sigmoid(logits)
        if diagonal:
            i = lax.broadcasted_iota(jnp.int32, sig.shape, 0) - yh * own
            j = lax.broadcasted_iota(jnp.int32, sig.shape, 1) - place * own
            sig = sig - ((i == j) & (i >= 0) & (i < own)).astype(F32)
        coef = (w_img[:, None] * w_txt[None, :] * 10.0 * sig).astype(BF)
        return blk, coef, contract(coef, all_img, (0, 0))

    blk_t, coef_t, part_t = pairs(txt_theirs, False)
    from_c = lax.ppermute(part_t.astype(BF), "c", SWAP)
    blk_m, coef_m, part_m = pairs(txt_mine, True)
    part_txt = (part_m + from_c.astype(F32)).astype(BF).reshape(near, own, width)
    grad_utxt = summed(lax.all_to_all(part_txt, NEAR, 0, 0))

    part_img = (
        jnp.dot(coef_m, blk_m, preferred_element_type=F32)
        + jnp.dot(coef_t, blk_t, preferred_element_type=F32)
    ).astype(BF)
    part_img = jnp.roll(part_img.reshape(nz, rows, width), lax.axis_index("z"), axis=0)
    sum_img = lax.psum_scatter(
        part_img.reshape(nz * rows, width), "z", scatter_dimension=0, tiled=True
    )

    txt_dot = jnp.sum(unit_txt * grad_utxt, axis=1, keepdims=True)
    grad_out = ((grad_utxt - unit_txt * txt_dot) * inv_txt).astype(BF)
    other = lax.ppermute(grad_out, "yh", SWAP)
    grad_full = jnp.concatenate(
        [jnp.where(low, grad_out, other), jnp.where(low, other, grad_out)], axis=0
    )
    grad_text = contract(grad_full, projection, (1, 1))

    weight_part = contract(text_feats, grad_full, (0, 0))
    top, bottom = weight_part[: half // 2], weight_part[half // 2 :]
    from_c = lax.ppermute(jnp.where(first, bottom, top).astype(BF), "c", SWAP)
    mine = (jnp.where(first, top, bottom) + from_c.astype(F32)).astype(BF)
    mine = mine.reshape(near, half // 2 // near, width)
    mine = summed(lax.all_to_all(mine, NEAR, 0, 0)).astype(BF)
    mine = summed(spread(mine, "z", nz)).astype(BF)
    mine, sum_img = lax.optimization_barrier((mine, sum_img))
    mine = spread(mine, NEAR, near).reshape(half // 2, width)
    theirs = lax.ppermute(mine, "c", SWAP)
    grad_weight = jnp.concatenate(
        [jnp.where(first, mine, theirs), jnp.where(first, theirs, mine)], axis=0
    ).astype(F32)

    left, right = sum_img[:, :half], sum_img[:, half:]
    from_yh = lax.ppermute(jnp.where(low, right, left), "yh", SWAP)
    grad_uimg = jnp.where(low, left, right).astype(F32) + from_yh.astype(F32)
    unit_img = images.astype(F32) * inv_img
    dot = jnp.sum(unit_img * grad_uimg, axis=1)
    dot = (dot + lax.ppermute(dot, "yh", SWAP))[:, None]
    grad_image = (grad_uimg - unit_img * dot) * inv_img
    return (grad_image, grad_text, grad_weight)


def solution(mesh):
    fine = Mesh(mesh.devices.reshape(SIZES), FINE)
    return jax.shard_map(
        on_device,
        mesh=fine,
        in_specs=(P(DP, "yh"), P(DP, "yh"), P("yh", None), P(DP)),
        out_specs=(P(DP, "yh"), P(DP, "yh"), P("yh", None)),
        check_vma=False,
    )
```

```python
import jax
import jax.numpy as jnp
import numpy as np
from jax import lax
from jax.experimental import pallas as pl
from jax.experimental.pallas import tpu as pltpu
from jax.sharding import Mesh
from jax.sharding import PartitionSpec as P

FINE = ("z", "x", "yl", "c", "yh")
SIZES = (8, 4, 2, 2, 2)
DP = ("z", "x", "yl", "c")
NEAR = ("x", "yl")
SWAP = [(0, 1), (1, 0)]
LANES = 128
CHUNK = 256
BF = jnp.bfloat16
F32 = jnp.float32


def contract(left, right, dims):
    return lax.dot_general(left, right, ((dims[:1], dims[1:]), ((), ())), preferred_element_type=F32)


def spread(block, axes, count):
    copies = jnp.broadcast_to(block[None], (count,) + block.shape)
    return lax.all_to_all(copies, axes, 0, 0)


def summed(got):
    return jnp.sum(got.astype(F32), axis=0)


def z_ring(block):
    n = SIZES[0]
    up = [(i, (i + 1) % n) for i in range(n)]
    down = [(i, (i - 1) % n) for i in range(n)]
    held = [None] * n
    held[0] = fro = to = block
    for step in range(1, n // 2):
        fro = held[n - step] = lax.ppermute(fro, "z", up)
        to = held[step] = lax.ppermute(to, "z", down)
    cut = block.shape[0] // 2
    held[n // 2] = (lax.ppermute(fro[:cut], "z", up), lax.ppermute(to[cut:], "z", down))
    return held


def with_column(block, weight):
    return jnp.concatenate([block, jnp.pad(weight[:, None], ((0, 0), (0, LANES - 1)))], axis=1)


def coefficients(txt, img, w_img, shift, out):
    width = img.shape[1]
    dots = contract(txt[:, :width], img[...], (1, 1))
    sig = 1.0 / (1.0 + jnp.exp(2.0 - 10.0 * dots))
    if shift is not None:
        row0, col0, own = shift
        i = lax.broadcasted_iota(jnp.int32, (1, dots.shape[1]), 1) - col0
        j = lax.broadcasted_iota(jnp.int32, (dots.shape[0], 1), 0) - row0
        i = jnp.where((i >= 0) & (i < own), i, -batch_far)
        sig = jnp.where(j == i, sig - 1.0, sig)
    w_txt = txt[:, width : width + 1].astype(F32) * 10.0
    coef = (w_txt * w_img * sig).astype(BF)
    out[...] = coef
    return coef


batch_far = 1 << 20


def theirs_kernel(*refs):
    blocks, (txt, img, w_img, coef, part) = refs[:-5], refs[-5:]
    width = img.shape[1]
    at = 0
    for block in blocks:
        n = block.shape[0]
        img[at : at + n] = block[:, :width]
        at += n
    pick = (lax.broadcasted_iota(jnp.int32, (8, LANES), 1) == 0).astype(BF)
    at = 0
    for block in blocks:
        n = block.shape[0]
        w_img[:, at : at + n] = contract(pick, block[:, width:], (1, 1))
        at += n
    for k in range(0, txt.shape[0], CHUNK):
        c = coefficients(txt.at[k : k + CHUNK], img, w_img[:1], None, coef.at[k : k + CHUNK])
        part[k : k + CHUNK] = jnp.dot(c, img[...], preferred_element_type=F32).astype(BF)


def mine_kernel(where, txt, img, w_img, coef, part):
    own = where[2]
    for k in range(0, txt.shape[0], CHUNK):
        shift = (where[0] * own - k, where[1] * own, own)
        c = coefficients(txt.at[k : k + CHUNK], img, w_img[:1], shift, coef.at[k : k + CHUNK])
        part[k : k + CHUNK] = jnp.dot(c, img[...], preferred_element_type=F32)


def image_kernel(where, coef_m, coef_t, txt_m, txt_t, part):
    n, width = part.shape[0], part.shape[2]
    rows = part.shape[1]
    per = CHUNK // rows
    for r in range(0, n, per):
        cols = slice(r * rows, (r + per) * rows)
        got = contract(coef_m[:, cols], txt_m[:, :width], (0, 0)) + contract(
            coef_t[:, cols], txt_t[:, :width], (0, 0)
        )
        for e in range(per):
            part[lax.rem(where[0] + r + e, n)] = got[e * rows : (e + 1) * rows].astype(BF)


def call(kernel, outs, scalars, *args):
    flops = 0
    for o in outs:
        flops += 2 * int(np.prod(o[0])) * 1024
    smem = [pl.BlockSpec(memory_space=pltpu.SMEM)] * (scalars is not None)
    lead = [scalars] * (scalars is not None)
    return pl.pallas_call(
        kernel,
        out_shape=[jax.ShapeDtypeStruct(*o) for o in outs],
        in_specs=smem + [pl.BlockSpec(memory_space=pltpu.VMEM)] * len(args),
        out_specs=[pl.BlockSpec(memory_space=pltpu.VMEM)] * len(outs),
        compiler_params=pltpu.CompilerParams(vmem_limit_bytes=28 << 20),
        cost_estimate=pl.CostEstimate(flops=flops, bytes_accessed=8 << 20, transcendentals=0),
    )(*lead, *args)


def on_device(images, text_feats, projection, ranks):
    rows, half = images.shape
    own = rows // 2
    width = 2 * half
    batch = rows * 128
    nz, near = 8, 8
    yh = lax.axis_index("yh")
    low = yh == 0
    first = lax.axis_index("c") == 0
    place = lax.axis_index("x") * 2 + lax.axis_index("yl")

    def side(array):
        return jnp.where(low, array[:own], array[own:])

    weight = (0.5 + 1.5 * ranks.astype(F32) / (batch - 1)).astype(BF)

    img_other = lax.ppermute(images, "yh", SWAP)
    partial = jnp.dot(text_feats, projection, preferred_element_type=F32)
    got = lax.ppermute(
        jnp.where(low, partial[own:], partial[:own]).astype(BF), "yh", SWAP
    )
    img32 = jnp.concatenate(
        [jnp.where(low, images, img_other), jnp.where(low, img_other, images)], axis=1
    ).astype(F32)
    inv_img = lax.rsqrt(jnp.sum(img32 * img32, axis=1, keepdims=True) + 1e-06)
    img_b = (img32 * inv_img).astype(BF)
    held = z_ring(with_column(img_b, weight))

    text_out = side(partial) + got.astype(F32)
    inv_txt = lax.rsqrt(jnp.sum(text_out * text_out, axis=1, keepdims=True) + 1e-06)
    unit_txt = text_out * inv_txt
    txt_mine = spread(with_column(unit_txt.astype(BF), side(weight)), NEAR, near)
    txt_mine = txt_mine.reshape(near * own, width + LANES)
    txt_theirs = lax.ppermute(txt_mine, "c", SWAP)

    blocks = jax.tree.leaves(held)
    n_img, n_txt = nz * rows, near * own
    coef_like = ((n_txt, n_img), BF)
    all_img, w_img, coef_t, part_t = call(
        theirs_kernel,
        [((n_img, width), BF), ((8, n_img), F32), coef_like, ((n_txt, width), BF)],
        None,
        *blocks,
        txt_theirs,
    )
    from_c = lax.ppermute(part_t, "c", SWAP)
    where = jnp.stack([place, yh, jnp.full_like(yh, own)]).astype(jnp.int32)
    coef_m, part_m = call(
        mine_kernel, [coef_like, ((n_txt, width), F32)], where, txt_mine, all_img, w_img
    )
    part_txt = (part_m + from_c.astype(F32)).astype(BF).reshape(near, own, width)
    grad_utxt = summed(lax.all_to_all(part_txt, NEAR, 0, 0))

    (part_img,) = call(
        image_kernel,
        [((nz, rows, width), BF)],
        lax.axis_index("z")[None].astype(jnp.int32),
        coef_m,
        coef_t,
        txt_mine,
        txt_theirs,
    )
    sum_img = lax.psum_scatter(
        part_img.reshape(nz * rows, width), "z", scatter_dimension=0, tiled=True
    )

    txt_dot = jnp.sum(unit_txt * grad_utxt, axis=1, keepdims=True)
    grad_out = ((grad_utxt - unit_txt * txt_dot) * inv_txt).astype(BF)
    other = lax.ppermute(grad_out, "yh", SWAP)
    grad_full = jnp.concatenate(
        [jnp.where(low, grad_out, other), jnp.where(low, other, grad_out)], axis=0
    )
    grad_text = contract(grad_full, projection, (1, 1))

    weight_part = contract(text_feats, grad_full, (0, 0))
    top, bottom = weight_part[: half // 2], weight_part[half // 2 :]
    from_c = lax.ppermute(jnp.where(first, bottom, top).astype(BF), "c", SWAP)
    mine = (jnp.where(first, top, bottom) + from_c.astype(F32)).astype(BF)
    mine = mine.reshape(near, half // 2 // near, width)
    mine = summed(lax.all_to_all(mine, NEAR, 0, 0)).astype(BF)
    mine, sum_img = lax.optimization_barrier((mine, sum_img))
    mine = summed(spread(mine, "z", nz)).astype(BF)
    mine = spread(mine, NEAR, near).reshape(half // 2, width)
    theirs = lax.ppermute(mine, "c", SWAP)
    grad_weight = jnp.concatenate(
        [jnp.where(first, mine, theirs), jnp.where(first, theirs, mine)], axis=0
    ).astype(F32)

    left, right = sum_img[:, :half], sum_img[:, half:]
    from_yh = lax.ppermute(jnp.where(low, right, left), "yh", SWAP)
    grad_uimg = jnp.where(low, left, right).astype(F32) + from_yh.astype(F32)
    unit_img = images.astype(F32) * inv_img
    dot = jnp.sum(unit_img * grad_uimg, axis=1)
    dot = (dot + lax.ppermute(dot, "yh", SWAP))[:, None]
    grad_image = (grad_uimg - unit_img * dot) * inv_img
    return (grad_image, grad_text, grad_weight)


def solution(mesh):
    fine = Mesh(mesh.devices.reshape(SIZES), FINE)
    return jax.shard_map(
        on_device,
        mesh=fine,
        in_specs=(P(DP, "yh"), P(DP, "yh"), P("yh", None), P(DP)),
        out_specs=(P(DP, "yh"), P(DP, "yh"), P("yh", None)),
        check_vma=False,
    )
```

```python
import functools

import jax
import jax.numpy as jnp
import numpy as np
from jax import lax
from jax.experimental import pallas as pl
from jax.experimental.pallas import tpu as pltpu
from jax.sharding import Mesh
from jax.sharding import PartitionSpec as P

FINE = ("z", "x", "yl", "c", "yh")
SIZES = (8, 4, 2, 2, 2)
DP = ("z", "x", "yl", "c")
NEAR = ("x", "yl")
SWAP = [(0, 1), (1, 0)]
LANES = 128
CHUNK = 256
BF = jnp.bfloat16
F32 = jnp.float32


def contract(left, right, dims):
    return lax.dot_general(left, right, ((dims[:1], dims[1:]), ((), ())), preferred_element_type=F32)


def spread(block, axes, count):
    copies = jnp.broadcast_to(block[None], (count,) + block.shape)
    return lax.all_to_all(copies, axes, 0, 0)


def summed(got):
    return jnp.sum(got.astype(F32), axis=0)


def with_column(block, weight):
    return jnp.concatenate([block, jnp.pad(weight[:, None], ((0, 0), (0, LANES - 1)))], axis=1)


def pair_kernel(where, img, txt_theirs, txt_mine, coef, theirs, mine, w_img):
    own, width = theirs.shape[1:]
    pick = (lax.broadcasted_iota(jnp.int32, (8, LANES), 1) == 0).astype(BF)
    w_img[...] = contract(pick, img[:, width:], (1, 1)) * 10.0
    half = txt_mine.shape[0]
    for txt, out, at in ((txt_theirs, theirs, 0), (txt_mine, mine, half)):
        for k in range(0, half, CHUNK):
            dots = contract(txt[k : k + CHUNK, :width], img[:, :width], (1, 1))
            sig = 1.0 / (1.0 + jnp.exp(2.0 - 10.0 * dots))
            if at:
                i = lax.broadcasted_iota(jnp.int32, (1, dots.shape[1]), 1) - where[0]
                j = lax.broadcasted_iota(jnp.int32, (dots.shape[0], 1), 0) - (where[1] - k)
                j = jnp.where((j >= 0) & (j < own), j, -1)
                i = jnp.where(i >= 0, i, -2)
                sig = jnp.where(j == i, sig - 1.0, sig)
            w_txt = txt[k : k + CHUNK, width : width + 1].astype(F32)
            c = (w_txt * w_img[:1] * sig).astype(BF)
            coef[at + k : at + k + CHUNK] = c
            got = jnp.dot(c, img[:, :width], preferred_element_type=F32).astype(BF)
            for e in range(0, CHUNK, own):
                out[(k + e) // own] = got[e : e + own]


def join_kernel(where, mine, theirs, out):
    n = mine.shape[0]
    out[pl.ds(pl.multiple_of(where[0] * n, 8), n)] = mine[...].astype(F32)
    out[pl.ds(pl.multiple_of((1 - where[0]) * n, 8), n)] = theirs[...].astype(F32)


def image_kernel(coef, txt_theirs, txt_mine, part):
    width = part.shape[1]
    half = txt_mine.shape[0]
    for r in range(0, part.shape[0], CHUNK):
        cut = slice(r, r + CHUNK)
        part[cut] = (
            contract(coef[:half, cut], txt_theirs[:, :width], (0, 0))
            + contract(coef[half:, cut], txt_mine[:, :width], (0, 0))
        ).astype(BF)


def call(kernel, outs, scalars, *args, scratch=(), flops=0):
    lead = [] if scalars is None else [jnp.stack(scalars).astype(jnp.int32)]
    return pl.pallas_call(
        kernel,
        out_shape=[jax.ShapeDtypeStruct(*o) for o in outs],
        in_specs=[pl.BlockSpec(memory_space=pltpu.SMEM)] * len(lead)
        + [pl.BlockSpec(memory_space=pltpu.VMEM)] * len(args),
        out_specs=[pl.BlockSpec(memory_space=pltpu.VMEM)] * len(outs),
        scratch_shapes=list(scratch),
        compiler_params=pltpu.CompilerParams(vmem_limit_bytes=16 << 20),
        cost_estimate=pl.CostEstimate(flops=flops, bytes_accessed=8 << 20, transcendentals=0),
    )(*lead, *args)


def on_device(images, text_feats, projection, ranks):
    rows, half = images.shape
    own = rows // 2
    width = 2 * half
    batch = rows * 128
    nz, near = 8, 8
    yh = lax.axis_index("yh")
    low = yh == 0
    first = lax.axis_index("c") == 0

    def side(array):
        return jnp.where(low, array[:own], array[own:])

    weight = (0.5 + 1.5 * ranks.astype(F32) / (batch - 1)).astype(BF)

    img_other = lax.ppermute(images, "yh", SWAP)
    partial = jnp.dot(text_feats, projection, preferred_element_type=F32)
    send = jnp.where(low, partial[own:], partial[:own]).astype(BF)
    send, img_other = lax.optimization_barrier((send, img_other))
    got = lax.ppermute(send, "yh", SWAP)
    img32 = jnp.concatenate(
        [jnp.where(low, images, img_other), jnp.where(low, img_other, images)], axis=1
    ).astype(F32)
    inv_img = lax.rsqrt(jnp.sum(img32 * img32, axis=1, keepdims=True) + 1e-06)
    img_b = (img32 * inv_img).astype(BF)

    text_out = side(partial) + got.astype(F32)
    inv_txt = lax.rsqrt(jnp.sum(text_out * text_out, axis=1, keepdims=True) + 1e-06)
    unit_txt = text_out * inv_txt
    all_img = lax.all_gather(with_column(img_b, weight), "z", axis=0, tiled=True)
    txt_block = with_column(unit_txt.astype(BF), side(weight))
    txt_mine = spread(txt_block, NEAR, near).reshape(near * own, width + LANES)
    txt_theirs = lax.ppermute(txt_mine, "c", SWAP)

    n_img, n_txt = nz * rows, near * own
    flops = 2 * n_img * 2 * n_txt * width
    coef, part_t, part_m = call(
        pair_kernel,
        [((2 * n_txt, n_img), BF), ((near, own, width), BF), ((near, own, width), BF)],
        [
            lax.axis_index("z") * rows + yh * own,
            (lax.axis_index("x") * 2 + lax.axis_index("yl")) * own,
        ],
        all_img,
        txt_theirs,
        txt_mine,
        scratch=[pltpu.VMEM((8, n_img), F32)],
        flops=2 * flops,
    )
    from_c = lax.ppermute(part_t, "c", SWAP)
    part_txt = (part_m.astype(F32) + from_c.astype(F32)).astype(BF)
    grad_utxt = summed(lax.all_to_all(part_txt, NEAR, 0, 0))

    (part_img,) = call(
        image_kernel, [((n_img, width), BF)], None, coef, txt_theirs, txt_mine, flops=flops
    )
    sum_img = lax.psum_scatter(part_img, "z", scatter_dimension=0, tiled=True)

    txt_dot = jnp.sum(unit_txt * grad_utxt, axis=1, keepdims=True)
    grad_out = ((grad_utxt - unit_txt * txt_dot) * inv_txt).astype(BF)
    other = lax.ppermute(grad_out, "yh", SWAP)
    grad_full = jnp.concatenate(
        [jnp.where(low, grad_out, other), jnp.where(low, other, grad_out)], axis=0
    )
    grad_text = contract(grad_full, projection, (1, 1))

    weight_part = contract(text_feats, grad_full, (0, 0))
    top, bottom = weight_part[: half // 2], weight_part[half // 2 :]
    from_c = lax.ppermute(jnp.where(first, bottom, top).astype(BF), "c", SWAP)
    mine = (jnp.where(first, top, bottom) + from_c.astype(F32)).astype(BF)
    mine = mine.reshape(near, half // 2 // near, width)
    mine = summed(lax.all_to_all(mine, NEAR, 0, 0)).astype(BF)
    mine, sum_img = lax.optimization_barrier((mine, sum_img))
    mine = summed(spread(mine, "z", nz)).astype(BF)

    left, right = sum_img[:, :half], sum_img[:, half:]
    from_yh = lax.ppermute(jnp.where(low, right, left), "yh", SWAP)
    grad_uimg = jnp.where(low, left, right).astype(F32) + from_yh.astype(F32)
    unit_img = images.astype(F32) * inv_img
    dot = jnp.sum(unit_img * grad_uimg, axis=1)
    dot_other = lax.ppermute(dot, "yh", SWAP)
    mine, dot_other = lax.optimization_barrier((mine, dot_other))
    grad_image = (grad_uimg - unit_img * (dot + dot_other)[:, None]) * inv_img

    mine = spread(mine, NEAR, near).reshape(half // 2, width)
    mine, grad_image, grad_text = lax.optimization_barrier((mine, grad_image, grad_text))
    theirs = lax.ppermute(mine, "c", SWAP)
    (grad_weight,) = call(
        join_kernel,
        [((half, width), F32)],
        [lax.axis_index("c")],
        mine,
        theirs,
    )
    return (grad_image, grad_text, grad_weight)


def solution(mesh):
    fine = Mesh(mesh.devices.reshape(SIZES), FINE)
    return jax.shard_map(
        on_device,
        mesh=fine,
        in_specs=(P(DP, "yh"), P(DP, "yh"), P("yh", None), P(DP)),
        out_specs=(P(DP, "yh"), P(DP, "yh"), P("yh", None)),
        check_vma=False,
    )
```

```python
import functools

import jax
import jax.numpy as jnp
import numpy as np
from jax import lax
from jax.experimental import pallas as pl
from jax.experimental.pallas import tpu as pltpu
from jax.sharding import Mesh
from jax.sharding import PartitionSpec as P

FINE = ("z", "x", "yl", "c", "yh")
SIZES = (8, 4, 2, 2, 2)
DP = ("z", "x", "yl", "c")
NEAR = ("x", "yl")
SWAP = [(0, 1), (1, 0)]
LANES = 128
CHUNK = 256
BF = jnp.bfloat16
F32 = jnp.float32


def contract(left, right, dims):
    return lax.dot_general(left, right, ((dims[:1], dims[1:]), ((), ())), preferred_element_type=F32)


def spread(block, axes, count):
    copies = jnp.broadcast_to(block[None], (count,) + block.shape)
    return lax.all_to_all(copies, axes, 0, 0)


def summed(got):
    return jnp.sum(got.astype(F32), axis=0)


def with_column(block, weight):
    return jnp.concatenate([block, jnp.pad(weight[:, None], ((0, 0), (0, LANES - 1)))], axis=1)


def pair_kernel(where, img, txt_theirs, txt_mine, coef, theirs, mine, w_img):
    own, width = theirs.shape[1:]
    pick = (lax.broadcasted_iota(jnp.int32, (8, LANES), 1) == 0).astype(BF)
    w_img[...] = contract(pick, img[:, width:], (1, 1)) * 10.0
    half = txt_mine.shape[0]
    for txt, out, at in ((txt_theirs, theirs, 0), (txt_mine, mine, half)):
        for k in range(0, half, CHUNK):
            dots = contract(txt[k : k + CHUNK, :width], img[:, :width], (1, 1))
            sig = 1.0 / (1.0 + jnp.exp(2.0 - 10.0 * dots))
            if at:
                i = lax.broadcasted_iota(jnp.int32, (1, dots.shape[1]), 1) - where[0]
                j = lax.broadcasted_iota(jnp.int32, (dots.shape[0], 1), 0) - (where[1] - k)
                j = jnp.where((j >= 0) & (j < own), j, -1)
                i = jnp.where(i >= 0, i, -2)
                sig = jnp.where(j == i, sig - 1.0, sig)
            w_txt = txt[k : k + CHUNK, width : width + 1].astype(F32)
            c = (w_txt * w_img[:1] * sig).astype(BF)
            coef[at + k : at + k + CHUNK] = c
            got = jnp.dot(c, img[:, :width], preferred_element_type=F32).astype(BF)
            for e in range(0, CHUNK, own):
                out[(k + e) // own] = got[e : e + own]


def join_kernel(where, mine, theirs, out):
    n = mine.shape[0]
    out[pl.ds(pl.multiple_of(where[0] * n, 8), n)] = mine[...].astype(F32)
    out[pl.ds(pl.multiple_of((1 - where[0]) * n, 8), n)] = theirs[...].astype(F32)


def image_kernel(coef, txt_theirs, txt_mine, part):
    width = part.shape[1]
    half = txt_mine.shape[0]
    for r in range(0, part.shape[0], CHUNK):
        cut = slice(r, r + CHUNK)
        part[cut] = (
            contract(coef[:half, cut], txt_theirs[:, :width], (0, 0))
            + contract(coef[half:, cut], txt_mine[:, :width], (0, 0))
        ).astype(BF)


def call(kernel, outs, scalars, *args, scratch=(), flops=0):
    lead = [] if scalars is None else [jnp.stack(scalars).astype(jnp.int32)]
    return pl.pallas_call(
        kernel,
        out_shape=[jax.ShapeDtypeStruct(*o) for o in outs],
        in_specs=[pl.BlockSpec(memory_space=pltpu.SMEM)] * len(lead)
        + [pl.BlockSpec(memory_space=pltpu.VMEM)] * len(args),
        out_specs=[pl.BlockSpec(memory_space=pltpu.VMEM)] * len(outs),
        scratch_shapes=list(scratch),
        compiler_params=pltpu.CompilerParams(vmem_limit_bytes=16 << 20),
        cost_estimate=pl.CostEstimate(flops=flops, bytes_accessed=8 << 20, transcendentals=0),
    )(*lead, *args)


def on_device(images, text_feats, projection, ranks):
    rows, half = images.shape
    own = rows // 2
    width = 2 * half
    batch = rows * 128
    nz, near = 8, 8
    yh = lax.axis_index("yh")
    low = yh == 0
    first = lax.axis_index("c") == 0

    def side(array):
        return jnp.where(low, array[:own], array[own:])

    weight = (0.5 + 1.5 * ranks.astype(F32) / (batch - 1)).astype(BF)

    img_other = lax.ppermute(images, "yh", SWAP)
    partial = jnp.dot(text_feats, projection, preferred_element_type=F32)
    send = jnp.where(low, partial[own:], partial[:own]).astype(BF)
    send, img_other = lax.optimization_barrier((send, img_other))
    got = lax.ppermute(send, "yh", SWAP)
    img32 = jnp.concatenate(
        [jnp.where(low, images, img_other), jnp.where(low, img_other, images)], axis=1
    ).astype(F32)
    inv_img = lax.rsqrt(jnp.sum(img32 * img32, axis=1, keepdims=True) + 1e-06)
    img_b = (img32 * inv_img).astype(BF)

    text_out = side(partial) + got.astype(F32)
    inv_txt = lax.rsqrt(jnp.sum(text_out * text_out, axis=1, keepdims=True) + 1e-06)
    unit_txt = text_out * inv_txt
    all_img = lax.all_gather(with_column(img_b, weight), "z", axis=0, tiled=True)
    txt_block = with_column(unit_txt.astype(BF), side(weight))
    txt_mine = spread(txt_block, NEAR, near).reshape(near * own, width + LANES)
    txt_theirs = lax.ppermute(txt_mine, "c", SWAP)

    n_img, n_txt = nz * rows, near * own
    flops = 2 * n_img * 2 * n_txt * width
    coef, part_t, part_m = call(
        pair_kernel,
        [((2 * n_txt, n_img), BF), ((near, own, width), BF), ((near, own, width), BF)],
        [
            lax.axis_index("z") * rows + yh * own,
            (lax.axis_index("x") * 2 + lax.axis_index("yl")) * own,
        ],
        all_img,
        txt_theirs,
        txt_mine,
        scratch=[pltpu.VMEM((8, n_img), F32)],
        flops=2 * flops,
    )
    from_c = lax.ppermute(part_t, "c", SWAP)
    part_txt = (part_m.astype(F32) + from_c.astype(F32)).astype(BF)
    grad_utxt = summed(lax.all_to_all(part_txt, NEAR, 0, 0))

    (part_img,) = call(
        image_kernel, [((n_img, width), BF)], None, coef, txt_theirs, txt_mine, flops=flops
    )
    sum_img = lax.psum_scatter(part_img, "z", scatter_dimension=0, tiled=True)

    txt_dot = jnp.sum(unit_txt * grad_utxt, axis=1, keepdims=True)
    grad_out = ((grad_utxt - unit_txt * txt_dot) * inv_txt).astype(BF)
    other = lax.ppermute(grad_out, "yh", SWAP)
    grad_full = jnp.concatenate(
        [jnp.where(low, grad_out, other), jnp.where(low, other, grad_out)], axis=0
    )
    grad_text = contract(grad_full, projection, (1, 1))

    weight_part = contract(text_feats, grad_full, (0, 0))
    top, bottom = weight_part[: half // 2], weight_part[half // 2 :]
    from_c = lax.ppermute(jnp.where(first, bottom, top).astype(BF), "c", SWAP)
    mine = (jnp.where(first, top, bottom) + from_c.astype(F32)).astype(BF)
    mine = mine.reshape(near, half // 2 // near, width)
    mine = summed(lax.all_to_all(mine, NEAR, 0, 0)).astype(BF)
    mine = summed(spread(mine, "z", nz)).astype(BF)

    left, right = sum_img[:, :half], sum_img[:, half:]
    from_yh = lax.ppermute(jnp.where(low, right, left), "yh", SWAP)
    grad_uimg = jnp.where(low, left, right).astype(F32) + from_yh.astype(F32)
    unit_img = images.astype(F32) * inv_img
    dot = jnp.sum(unit_img * grad_uimg, axis=1)
    dot_other = lax.ppermute(dot, "yh", SWAP)
    mine, dot_other = lax.optimization_barrier((mine, dot_other))
    grad_image = (grad_uimg - unit_img * (dot + dot_other)[:, None]) * inv_img

    mine = spread(mine, NEAR, near).reshape(half // 2, width)
    mine, grad_image, grad_text = lax.optimization_barrier((mine, grad_image, grad_text))
    theirs = lax.ppermute(mine, "c", SWAP)
    (grad_weight,) = call(
        join_kernel,
        [((half, width), F32)],
        [lax.axis_index("c")],
        mine,
        theirs,
    )
    return (grad_image, grad_text, grad_weight)


def solution(mesh):
    fine = Mesh(mesh.devices.reshape(SIZES), FINE)
    return jax.shard_map(
        on_device,
        mesh=fine,
        in_specs=(P(DP, "yh"), P(DP, "yh"), P("yh", None), P(DP)),
        out_specs=(P(DP, "yh"), P(DP, "yh"), P("yh", None)),
        check_vma=False,
    )
```

```python
import functools

import jax
import jax.numpy as jnp
import numpy as np
from jax import lax
from jax.experimental import pallas as pl
from jax.experimental.pallas import tpu as pltpu
from jax.sharding import Mesh
from jax.sharding import PartitionSpec as P

FINE = ("z", "x", "yl", "c", "yh")
SIZES = (8, 4, 2, 2, 2)
DP = ("z", "x", "yl", "c")
NEAR = ("x", "yl")
SWAP = [(0, 1), (1, 0)]
LANES = 128
CHUNK = 256
BF = jnp.bfloat16
F32 = jnp.float32


def contract(left, right, dims):
    return lax.dot_general(left, right, ((dims[:1], dims[1:]), ((), ())), preferred_element_type=F32)


def spread(block, axes, count):
    copies = jnp.broadcast_to(block[None], (count,) + block.shape)
    return lax.all_to_all(copies, axes, 0, 0)


def summed(got):
    return jnp.sum(got.astype(F32), axis=0)


def with_column(block, weight):
    return jnp.concatenate([block, jnp.pad(weight[:, None], ((0, 0), (0, LANES - 1)))], axis=1)


def pair_kernel(has_own, where, img, txt, coef, part, w_img):
    own, width = part.shape[1:]
    pick = (lax.broadcasted_iota(jnp.int32, (8, LANES), 1) == 0).astype(BF)
    w_img[...] = contract(pick, img[:, width:], (1, 1)) * 10.0
    for k in range(0, txt.shape[0], CHUNK):
        dots = contract(txt[k : k + CHUNK, :width], img[:, :width], (1, 1))
        sig = 1.0 / (1.0 + jnp.exp(2.0 - 10.0 * dots))
        if has_own:
            i = lax.broadcasted_iota(jnp.int32, (1, dots.shape[1]), 1) - where[0]
            j = lax.broadcasted_iota(jnp.int32, (dots.shape[0], 1), 0) - (where[1] - k)
            j = jnp.where((j >= 0) & (j < own), j, -1)
            i = jnp.where(i >= 0, i, -2)
            sig = jnp.where(j == i, sig - 1.0, sig)
        w_txt = txt[k : k + CHUNK, width : width + 1].astype(F32)
        c = (w_txt * w_img[:1] * sig).astype(BF)
        coef[k : k + CHUNK] = c
        got = jnp.dot(c, img[:, :width], preferred_element_type=F32).astype(BF)
        for e in range(0, CHUNK, own):
            part[(k + e) // own] = got[e : e + own]


def ending_kernel(got, unit, inv, grad_out):
    grad = got[0].astype(F32)
    for k in range(1, got.shape[0]):
        grad = grad + got[k].astype(F32)
    dot = jnp.sum(unit[...] * grad, axis=1, keepdims=True)
    grad_out[...] = ((grad - unit[...] * dot) * inv[...]).astype(BF)


def join_kernel(where, mine, theirs, out):
    n = mine.shape[0]
    out[pl.ds(pl.multiple_of(where[0] * n, 8), n)] = mine[...].astype(F32)
    out[pl.ds(pl.multiple_of((1 - where[0]) * n, 8), n)] = theirs[...].astype(F32)


def image_kernel(coef_t, coef_m, txt_theirs, txt_mine, part):
    width = part.shape[1]
    for r in range(0, part.shape[0], CHUNK):
        cut = slice(r, r + CHUNK)
        part[cut] = (
            contract(coef_t[:, cut], txt_theirs[:, :width], (0, 0))
            + contract(coef_m[:, cut], txt_mine[:, :width], (0, 0))
        ).astype(BF)


def call(kernel, outs, scalars, *args, scratch=(), flops=0):
    lead = [] if scalars is None else [jnp.stack(scalars).astype(jnp.int32)]
    return pl.pallas_call(
        kernel,
        out_shape=[jax.ShapeDtypeStruct(*o) for o in outs],
        in_specs=[pl.BlockSpec(memory_space=pltpu.SMEM)] * len(lead)
        + [pl.BlockSpec(memory_space=pltpu.VMEM)] * len(args),
        out_specs=[pl.BlockSpec(memory_space=pltpu.VMEM)] * len(outs),
        scratch_shapes=list(scratch),
        compiler_params=pltpu.CompilerParams(vmem_limit_bytes=16 << 20),
        cost_estimate=pl.CostEstimate(flops=flops, bytes_accessed=8 << 20, transcendentals=0),
    )(*lead, *args)


def on_device(images, text_feats, projection, ranks):
    rows, half = images.shape
    own = rows // 2
    width = 2 * half
    batch = rows * 128
    nz, near = 8, 8
    yh = lax.axis_index("yh")
    low = yh == 0
    first = lax.axis_index("c") == 0

    def side(array):
        return jnp.where(low, array[:own], array[own:])

    weight = (0.5 + 1.5 * ranks.astype(F32) / (batch - 1)).astype(BF)

    img_other = lax.ppermute(images, "yh", SWAP)
    partial = jnp.dot(text_feats, projection, preferred_element_type=F32)
    send = jnp.where(low, partial[own:], partial[:own]).astype(BF)
    send, img_other = lax.optimization_barrier((send, img_other))
    got = lax.ppermute(send, "yh", SWAP)
    img32 = jnp.concatenate(
        [jnp.where(low, images, img_other), jnp.where(low, img_other, images)], axis=1
    ).astype(F32)
    inv_img = lax.rsqrt(jnp.sum(img32 * img32, axis=1, keepdims=True) + 1e-06)
    img_b = (img32 * inv_img).astype(BF)

    text_out = side(partial) + got.astype(F32)
    inv_txt = lax.rsqrt(jnp.sum(text_out * text_out, axis=1, keepdims=True) + 1e-06)
    unit_txt = text_out * inv_txt
    all_img = lax.all_gather(with_column(img_b, weight), "z", axis=0, tiled=True)
    txt_block = with_column(unit_txt.astype(BF), side(weight))
    txt_mine = spread(txt_block, NEAR, near).reshape(near * own, width + LANES)
    txt_theirs = lax.ppermute(txt_mine, "c", SWAP)

    n_img, n_txt = nz * rows, near * own
    flops = 2 * n_img * 2 * n_txt * width
    ids = [
        lax.axis_index("z") * rows + yh * own,
        (lax.axis_index("x") * 2 + lax.axis_index("yl")) * own,
    ]

    def pairs(txt, has_own):
        return call(
            functools.partial(pair_kernel, has_own),
            [((n_txt, n_img), BF), ((near, own, width), BF)],
            ids,
            all_img,
            txt,
            scratch=[pltpu.VMEM((8, n_img), F32)],
            flops=flops,
        )

    coef_t, part_t = pairs(txt_theirs, False)
    from_c = lax.ppermute(part_t, "c", SWAP)
    coef_m, part_m = pairs(txt_mine, True)
    part_txt = (part_m.astype(F32) + from_c.astype(F32)).astype(BF)
    got = lax.all_to_all(part_txt, NEAR, 0, 0)

    (part_img,) = call(
        image_kernel, [((n_img, width), BF)], None, coef_t, coef_m, txt_theirs, txt_mine, flops=flops
    )
    sum_img = lax.psum_scatter(part_img, "z", scatter_dimension=0, tiled=True)

    (grad_out,) = call(ending_kernel, [((own, width), BF)], None, got, unit_txt, inv_txt)
    other = lax.ppermute(grad_out, "yh", SWAP)
    grad_full = jnp.concatenate(
        [jnp.where(low, grad_out, other), jnp.where(low, other, grad_out)], axis=0
    )
    grad_text = contract(grad_full, projection, (1, 1))

    weight_part = contract(text_feats, grad_full, (0, 0))
    top, bottom = weight_part[: half // 2], weight_part[half // 2 :]
    from_c = lax.ppermute(jnp.where(first, bottom, top).astype(BF), "c", SWAP)
    mine = (jnp.where(first, top, bottom) + from_c.astype(F32)).astype(BF)
    mine = mine.reshape(near, half // 2 // near, width)
    mine = summed(lax.all_to_all(mine, NEAR, 0, 0)).astype(BF)
    mine = summed(spread(mine, "z", nz)).astype(BF)

    left, right = sum_img[:, :half], sum_img[:, half:]
    from_yh = lax.ppermute(jnp.where(low, right, left), "yh", SWAP)
    grad_uimg = jnp.where(low, left, right).astype(F32) + from_yh.astype(F32)
    unit_img = images.astype(F32) * inv_img
    dot = jnp.sum(unit_img * grad_uimg, axis=1)
    dot_other = lax.ppermute(dot, "yh", SWAP)
    mine, dot_other = lax.optimization_barrier((mine, dot_other))
    grad_image = (grad_uimg - unit_img * (dot + dot_other)[:, None]) * inv_img

    mine = spread(mine, NEAR, near).reshape(half // 2, width)
    mine, grad_image, grad_text = lax.optimization_barrier((mine, grad_image, grad_text))
    theirs = lax.ppermute(mine, "c", SWAP)
    (grad_weight,) = call(
        join_kernel,
        [((half, width), F32)],
        [lax.axis_index("c")],
        mine,
        theirs,
    )
    return (grad_image, grad_text, grad_weight)


def solution(mesh):
    fine = Mesh(mesh.devices.reshape(SIZES), FINE)
    return jax.shard_map(
        on_device,
        mesh=fine,
        in_specs=(P(DP, "yh"), P(DP, "yh"), P("yh", None), P(DP)),
        out_specs=(P(DP, "yh"), P(DP, "yh"), P("yh", None)),
        check_vma=False,
    )
```

```python
import functools

import jax
import jax.numpy as jnp
import numpy as np
from jax import lax
from jax.experimental import pallas as pl
from jax.experimental.pallas import tpu as pltpu
from jax.sharding import Mesh
from jax.sharding import PartitionSpec as P

FINE = ("z", "x", "yl", "c", "yh")
SIZES = (8, 4, 2, 2, 2)
DP = ("z", "x", "yl", "c")
NEAR = ("x", "yl")
SWAP = [(0, 1), (1, 0)]
LANES = 128
CHUNK = 256
BF = jnp.bfloat16
F32 = jnp.float32


def contract(left, right, dims):
    return lax.dot_general(left, right, ((dims[:1], dims[1:]), ((), ())), preferred_element_type=F32)


def spread(block, axes, count):
    copies = jnp.broadcast_to(block[None], (count,) + block.shape)
    return lax.all_to_all(copies, axes, 0, 0)


def summed(got):
    return jnp.sum(got.astype(F32), axis=0)


def with_column(block, weight):
    return jnp.concatenate([block, jnp.pad(weight[:, None], ((0, 0), (0, LANES - 1)))], axis=1)


def pair_kernel(has_own, where, img, txt, coef, part, w_img):
    own, width = part.shape[1:]
    pick = (lax.broadcasted_iota(jnp.int32, (8, LANES), 1) == 0).astype(BF)
    w_img[...] = contract(pick, img[:, width:], (1, 1)) * 10.0
    for k in range(0, txt.shape[0], CHUNK):
        dots = contract(txt[k : k + CHUNK, :width], img[:, :width], (1, 1))
        sig = 1.0 / (1.0 + jnp.exp(2.0 - 10.0 * dots))
        if has_own:
            i = lax.broadcasted_iota(jnp.int32, (1, dots.shape[1]), 1) - where[0]
            j = lax.broadcasted_iota(jnp.int32, (dots.shape[0], 1), 0) - (where[1] - k)
            j = jnp.where((j >= 0) & (j < own), j, -1)
            i = jnp.where(i >= 0, i, -2)
            sig = jnp.where(j == i, sig - 1.0, sig)
        w_txt = txt[k : k + CHUNK, width : width + 1].astype(F32)
        c = (w_txt * w_img[:1] * sig).astype(BF)
        coef[k : k + CHUNK] = c
        got = jnp.dot(c, img[:, :width], preferred_element_type=F32).astype(BF)
        for e in range(0, CHUNK, own):
            part[(k + e) // own] = got[e : e + own]


def ending_kernel(got, unit, inv, grad_out):
    grad = got[0].astype(F32)
    for k in range(1, got.shape[0]):
        grad = grad + got[k].astype(F32)
    dot = jnp.sum(unit[...] * grad, axis=1, keepdims=True)
    grad_out[...] = ((grad - unit[...] * dot) * inv[...]).astype(BF)


def join_kernel(where, mine, theirs, out):
    n = mine.shape[0]
    out[pl.ds(pl.multiple_of(where[0] * n, 8), n)] = mine[...].astype(F32)
    out[pl.ds(pl.multiple_of((1 - where[0]) * n, 8), n)] = theirs[...].astype(F32)


def image_kernel(coef_t, coef_m, txt_theirs, txt_mine, part):
    width = part.shape[1]
    for r in range(0, part.shape[0], CHUNK):
        cut = slice(r, r + CHUNK)
        part[cut] = (
            contract(coef_t[:, cut], txt_theirs[:, :width], (0, 0))
            + contract(coef_m[:, cut], txt_mine[:, :width], (0, 0))
        ).astype(BF)


def call(kernel, outs, scalars, *args, scratch=(), flops=0):
    lead = [] if scalars is None else [jnp.stack(scalars).astype(jnp.int32)]
    return pl.pallas_call(
        kernel,
        out_shape=[jax.ShapeDtypeStruct(*o) for o in outs],
        in_specs=[pl.BlockSpec(memory_space=pltpu.SMEM)] * len(lead)
        + [pl.BlockSpec(memory_space=pltpu.VMEM)] * len(args),
        out_specs=[pl.BlockSpec(memory_space=pltpu.VMEM)] * len(outs),
        scratch_shapes=list(scratch),
        compiler_params=pltpu.CompilerParams(vmem_limit_bytes=16 << 20),
        cost_estimate=pl.CostEstimate(flops=flops, bytes_accessed=8 << 20, transcendentals=0),
    )(*lead, *args)


def on_device(images, text_feats, projection, ranks):
    rows, half = images.shape
    own = rows // 2
    width = 2 * half
    batch = rows * 128
    nz, near = 8, 8
    yh = lax.axis_index("yh")
    low = yh == 0
    first = lax.axis_index("c") == 0

    def side(array):
        return jnp.where(low, array[:own], array[own:])

    weight = (0.5 + 1.5 * ranks.astype(F32) / (batch - 1)).astype(BF)

    img_other = lax.ppermute(images, "yh", SWAP)
    partial = jnp.dot(text_feats, projection, preferred_element_type=F32)
    send = jnp.where(low, partial[own:], partial[:own]).astype(BF)
    send, img_other = lax.optimization_barrier((send, img_other))
    got = lax.ppermute(send, "yh", SWAP)
    img32 = jnp.concatenate(
        [jnp.where(low, images, img_other), jnp.where(low, img_other, images)], axis=1
    ).astype(F32)
    inv_img = lax.rsqrt(jnp.sum(img32 * img32, axis=1, keepdims=True) + 1e-06)
    img_b = (img32 * inv_img).astype(BF)

    text_out = side(partial) + got.astype(F32)
    inv_txt = lax.rsqrt(jnp.sum(text_out * text_out, axis=1, keepdims=True) + 1e-06)
    unit_txt = text_out * inv_txt
    all_img = lax.all_gather(with_column(img_b, weight), "z", axis=0, tiled=True)
    txt_block = with_column(unit_txt.astype(BF), side(weight))
    txt_mine = spread(txt_block, NEAR, near).reshape(near * own, width + LANES)
    txt_theirs = lax.ppermute(txt_mine, "c", SWAP)

    n_img, n_txt = nz * rows, near * own
    flops = 2 * n_img * 2 * n_txt * width
    ids = [
        lax.axis_index("z") * rows + yh * own,
        (lax.axis_index("x") * 2 + lax.axis_index("yl")) * own,
    ]

    def pairs(txt, has_own):
        return call(
            functools.partial(pair_kernel, has_own),
            [((n_txt, n_img), BF), ((near, own, width), BF)],
            ids,
            all_img,
            txt,
            scratch=[pltpu.VMEM((8, n_img), F32)],
            flops=flops,
        )

    coef_t, part_t = pairs(txt_theirs, False)
    from_c = lax.ppermute(part_t, "c", SWAP)
    coef_m, part_m = pairs(txt_mine, True)
    part_txt = (part_m.astype(F32) + from_c.astype(F32)).astype(BF)
    got = lax.all_to_all(part_txt, NEAR, 0, 0)

    (part_img,) = call(
        image_kernel, [((n_img, width), BF)], None, coef_t, coef_m, txt_theirs, txt_mine, flops=flops
    )
    sum_img = lax.psum_scatter(part_img, "z", scatter_dimension=0, tiled=True)

    (grad_out,) = call(ending_kernel, [((own, width), BF)], None, got, unit_txt, inv_txt)
    other = lax.ppermute(grad_out, "yh", SWAP)
    grad_full = jnp.concatenate(
        [jnp.where(low, grad_out, other), jnp.where(low, other, grad_out)], axis=0
    )
    grad_text = contract(grad_full, projection, (1, 1))

    weight_part = contract(text_feats, grad_full, (0, 0))
    top, bottom = weight_part[: half // 2], weight_part[half // 2 :]
    from_c = lax.ppermute(jnp.where(first, bottom, top).astype(BF), "c", SWAP)
    mine = (jnp.where(first, top, bottom) + from_c.astype(F32)).astype(BF)
    mine = mine.reshape(near, half // 2 // near, width)
    mine = summed(lax.all_to_all(mine, NEAR, 0, 0)).astype(BF)
    mine = summed(spread(mine, "z", nz)).astype(BF)

    from_yh = lax.ppermute(sum_img, "yh", SWAP)
    mine, from_yh = lax.optimization_barrier((mine, from_yh))
    grad_uimg = sum_img.astype(F32) + from_yh.astype(F32)
    dot = jnp.sum(img32 * grad_uimg, axis=1, keepdims=True) * inv_img
    grad_uimg = jnp.where(low, grad_uimg[:, :half], grad_uimg[:, half:])
    grad_image = (grad_uimg - images.astype(F32) * inv_img * dot) * inv_img

    mine = spread(mine, NEAR, near).reshape(half // 2, width)
    mine, grad_image, grad_text = lax.optimization_barrier((mine, grad_image, grad_text))
    theirs = lax.ppermute(mine, "c", SWAP)
    (grad_weight,) = call(
        join_kernel,
        [((half, width), F32)],
        [lax.axis_index("c")],
        mine,
        theirs,
    )
    return (grad_image, grad_text, grad_weight)


def solution(mesh):
    fine = Mesh(mesh.devices.reshape(SIZES), FINE)
    return jax.shard_map(
        on_device,
        mesh=fine,
        in_specs=(P(DP, "yh"), P(DP, "yh"), P("yh", None), P(DP)),
        out_specs=(P(DP, "yh"), P(DP, "yh"), P("yh", None)),
        check_vma=False,
    )
```

```python
import functools

import jax
import jax.numpy as jnp
import numpy as np
from jax import lax
from jax.experimental import pallas as pl
from jax.experimental.pallas import tpu as pltpu
from jax.sharding import Mesh
from jax.sharding import PartitionSpec as P

FINE = ("z", "x", "yl", "c", "yh")
SIZES = (8, 4, 2, 2, 2)
DP = ("z", "x", "yl", "c")
NEAR = ("x", "yl")
SWAP = [(0, 1), (1, 0)]
LANES = 128
CHUNK = 256
TEXTS = 512
BF = jnp.bfloat16
F32 = jnp.float32


def contract(left, right, dims):
    return lax.dot_general(left, right, ((dims[:1], dims[1:]), ((), ())), preferred_element_type=F32)


def spread(block, axes, count):
    copies = jnp.broadcast_to(block[None], (count,) + block.shape)
    return lax.all_to_all(copies, axes, 0, 0)


def summed(got):
    return jnp.sum(got.astype(F32), axis=0)


def with_column(block, weight):
    return jnp.concatenate([block, jnp.pad(weight[:, None], ((0, 0), (0, LANES - 1)))], axis=1)


def pair_kernel(has_own, where, img, txt, coef, part, w_img):
    own, width = part.shape[1:]
    pick = (lax.broadcasted_iota(jnp.int32, (8, LANES), 1) == 0).astype(BF)
    w_img[...] = contract(pick, img[:, width:], (1, 1)) * 10.0
    for k in range(0, txt.shape[0], TEXTS):
        dots = contract(txt[k : k + TEXTS, :width], img[:, :width], (1, 1))
        sig = 1.0 / (1.0 + jnp.exp(2.0 - 10.0 * dots))
        if has_own:
            i = lax.broadcasted_iota(jnp.int32, (1, dots.shape[1]), 1) - where[0]
            j = lax.broadcasted_iota(jnp.int32, (dots.shape[0], 1), 0) - (where[1] - k)
            j = jnp.where((j >= 0) & (j < own), j, -1)
            i = jnp.where(i >= 0, i, -2)
            sig = jnp.where(j == i, sig - 1.0, sig)
        w_txt = txt[k : k + TEXTS, width : width + 1].astype(F32)
        c = (w_txt * w_img[:1] * sig).astype(BF)
        coef[k : k + TEXTS] = c
        got = jnp.dot(c, img[:, :width], preferred_element_type=F32).astype(BF)
        for e in range(0, TEXTS, own):
            part[(k + e) // own] = got[e : e + own]


def ending_kernel(got, unit, inv, grad_out):
    grad = got[0].astype(F32)
    for k in range(1, got.shape[0]):
        grad = grad + got[k].astype(F32)
    dot = jnp.sum(unit[...] * grad, axis=1, keepdims=True)
    grad_out[...] = ((grad - unit[...] * dot) * inv[...]).astype(BF)


def join_kernel(where, mine, theirs, out):
    n = mine.shape[0]
    out[pl.ds(pl.multiple_of(where[0] * n, 8), n)] = mine[...].astype(F32)
    out[pl.ds(pl.multiple_of((1 - where[0]) * n, 8), n)] = theirs[...].astype(F32)


def image_kernel(coef_t, coef_m, txt_theirs, txt_mine, part):
    width = part.shape[1]
    for r in range(0, part.shape[0], CHUNK):
        cut = slice(r, r + CHUNK)
        part[cut] = (
            contract(coef_t[:, cut], txt_theirs[:, :width], (0, 0))
            + contract(coef_m[:, cut], txt_mine[:, :width], (0, 0))
        ).astype(BF)


def call(kernel, outs, scalars, *args, scratch=(), flops=0):
    lead = [] if scalars is None else [jnp.stack(scalars).astype(jnp.int32)]
    return pl.pallas_call(
        kernel,
        out_shape=[jax.ShapeDtypeStruct(*o) for o in outs],
        in_specs=[pl.BlockSpec(memory_space=pltpu.SMEM)] * len(lead)
        + [pl.BlockSpec(memory_space=pltpu.VMEM)] * len(args),
        out_specs=[pl.BlockSpec(memory_space=pltpu.VMEM)] * len(outs),
        scratch_shapes=list(scratch),
        compiler_params=pltpu.CompilerParams(vmem_limit_bytes=16 << 20),
        cost_estimate=pl.CostEstimate(flops=flops, bytes_accessed=8 << 20, transcendentals=0),
    )(*lead, *args)


def on_device(images, text_feats, projection, ranks):
    rows, half = images.shape
    own = rows // 2
    width = 2 * half
    batch = rows * 128
    nz, near = 8, 8
    yh = lax.axis_index("yh")
    low = yh == 0
    first = lax.axis_index("c") == 0

    def side(array):
        return jnp.where(low, array[:own], array[own:])

    weight = (0.5 + 1.5 * ranks.astype(F32) / (batch - 1)).astype(BF)

    img_other = lax.ppermute(images, "yh", SWAP)
    partial = jnp.dot(text_feats, projection, preferred_element_type=F32)
    send = jnp.where(low, partial[own:], partial[:own]).astype(BF)
    send, img_other = lax.optimization_barrier((send, img_other))
    got = lax.ppermute(send, "yh", SWAP)
    img32 = jnp.concatenate(
        [jnp.where(low, images, img_other), jnp.where(low, img_other, images)], axis=1
    ).astype(F32)
    inv_img = lax.rsqrt(jnp.sum(img32 * img32, axis=1, keepdims=True) + 1e-06)
    img_b = (img32 * inv_img).astype(BF)

    text_out = side(partial) + got.astype(F32)
    inv_txt = lax.rsqrt(jnp.sum(text_out * text_out, axis=1, keepdims=True) + 1e-06)
    unit_txt = text_out * inv_txt
    all_img = lax.all_gather(with_column(img_b, weight), "z", axis=0, tiled=True)
    txt_block = with_column(unit_txt.astype(BF), side(weight))
    txt_mine = spread(txt_block, NEAR, near).reshape(near * own, width + LANES)
    txt_theirs = lax.ppermute(txt_mine, "c", SWAP)

    n_img, n_txt = nz * rows, near * own
    flops = 2 * n_img * 2 * n_txt * width
    ids = [
        lax.axis_index("z") * rows + yh * own,
        (lax.axis_index("x") * 2 + lax.axis_index("yl")) * own,
    ]

    def pairs(txt, has_own):
        return call(
            functools.partial(pair_kernel, has_own),
            [((n_txt, n_img), BF), ((near, own, width), BF)],
            ids,
            all_img,
            txt,
            scratch=[pltpu.VMEM((8, n_img), F32)],
            flops=flops,
        )

    coef_t, part_t = pairs(txt_theirs, False)
    from_c = lax.ppermute(part_t, "c", SWAP)
    coef_m, part_m = pairs(txt_mine, True)
    part_txt = (part_m.astype(F32) + from_c.astype(F32)).astype(BF)
    got = lax.all_to_all(part_txt, NEAR, 0, 0)

    (part_img,) = call(
        image_kernel, [((n_img, width), BF)], None, coef_t, coef_m, txt_theirs, txt_mine, flops=flops
    )
    sum_img = lax.psum_scatter(part_img, "z", scatter_dimension=0, tiled=True)

    (grad_out,) = call(ending_kernel, [((own, width), BF)], None, got, unit_txt, inv_txt)
    other = lax.ppermute(grad_out, "yh", SWAP)
    grad_full = jnp.concatenate(
        [jnp.where(low, grad_out, other), jnp.where(low, other, grad_out)], axis=0
    )
    grad_text = contract(grad_full, projection, (1, 1))

    weight_part = contract(text_feats, grad_full, (0, 0))
    top, bottom = weight_part[: half // 2], weight_part[half // 2 :]
    from_c = lax.ppermute(jnp.where(first, bottom, top).astype(BF), "c", SWAP)
    mine = (jnp.where(first, top, bottom) + from_c.astype(F32)).astype(BF)
    mine = mine.reshape(near, half // 2 // near, width)
    mine = summed(lax.all_to_all(mine, NEAR, 0, 0)).astype(BF)
    mine = summed(spread(mine, "z", nz)).astype(BF)

    left, right = sum_img[:, :half], sum_img[:, half:]
    from_yh = lax.ppermute(jnp.where(low, right, left), "yh", SWAP)
    grad_uimg = jnp.where(low, left, right).astype(F32) + from_yh.astype(F32)
    unit_img = images.astype(F32) * inv_img
    dot = jnp.sum(unit_img * grad_uimg, axis=1)
    dot_other = lax.ppermute(dot, "yh", SWAP)
    mine, dot_other = lax.optimization_barrier((mine, dot_other))
    grad_image = (grad_uimg - unit_img * (dot + dot_other)[:, None]) * inv_img

    mine = spread(mine, NEAR, near).reshape(half // 2, width)
    mine, grad_image, grad_text = lax.optimization_barrier((mine, grad_image, grad_text))
    theirs = lax.ppermute(mine, "c", SWAP)
    (grad_weight,) = call(
        join_kernel,
        [((half, width), F32)],
        [lax.axis_index("c")],
        mine,
        theirs,
    )
    return (grad_image, grad_text, grad_weight)


def solution(mesh):
    fine = Mesh(mesh.devices.reshape(SIZES), FINE)
    return jax.shard_map(
        on_device,
        mesh=fine,
        in_specs=(P(DP, "yh"), P(DP, "yh"), P("yh", None), P(DP)),
        out_specs=(P(DP, "yh"), P(DP, "yh"), P("yh", None)),
        check_vma=False,
    )
```
